32 devices in a mesh: seq: 8 (over y, x, core), head: 4 (over z).
Axes of the slice: x: 2, y: 2, z: 4, core: 2. Of those that a mesh axis runs over, the one named last changes fastest.
Arguments:
- query: bfloat16 [4096, 7168], P(('seq', 'head')), may hold values from -16 to 16
- key: bfloat16 [4096, 7168], P(('seq', 'head')), may hold values from -16 to 16
- value: bfloat16 [4096, 7168], P(('seq', 'head')), may hold values from -8 to 8
- exponent: int32 [64], replicated, may hold values from 1 to 64, as said below
Outputs:
- attended: bfloat16 [4096, 7168], P(('seq', 'head'))
The draws below stay inside these ranges and needn't reach their ends.
Inputs may be any that keep to these rules, and one draw needn't show every extreme that they name: Head h (counted from 0) has an exponent within 6 of h + 1; head 0 has 1 and the last head has 64.
All inputs are finite; a program needn't handle non-finite values.
Results may differ from the reference program's by a relative error of at most 0.0033.
Values may be sent and summed in bfloat16 or wider, within the bound.
No kernel may reach another device: no remote copies, remote signals or barrier semaphores. Data moves between devices by JAX's collectives and lax.ppermute only.
A program may use at most 128 MiB of HBM per device.

```python
import jax
import jax.numpy as jnp
from jax import lax

HEADS = 64
HS = 112
D = 7168
BLOCK = 128
MIN_BAND = 16
MAX_BAND = 40
TOKENS = 4096


def exponent_draw(key):
    jitter = jax.random.randint(jax.random.fold_in(key, 301), (HEADS,), -6, 7)
    ranks = jnp.arange(HEADS, dtype=jnp.int32)
    drawn = jnp.clip(ranks + 1 + jitter, 1, HEADS)
    drawn = jnp.where(ranks == 0, 1, drawn)
    drawn = jnp.where(ranks == HEADS - 1, HEADS, drawn)
    return drawn.astype(jnp.int32)


def paired_draw(key):
    first_key = jax.random.fold_in(key, 101)
    second_key = jax.random.fold_in(key, 102)
    queries = jnp.clip(jax.random.normal(first_key, (TOKENS, D), jnp.float32), -6.0, 6.0)
    keys_drawn = jnp.clip(jax.random.normal(second_key, (TOKENS, D), jnp.float32), -6.0, 6.0)
    return (queries, keys_drawn)


def draw_query(key, part):
    return paired_draw(key)[0].astype(jnp.bfloat16)


def draw_key(key, part):
    return paired_draw(key)[1].astype(jnp.bfloat16)


def draw_value(key, part):
    noise_key = jax.random.fold_in(key, 201)
    offset_key = jax.random.fold_in(key, 202)
    offsets = jax.random.uniform(offset_key, (TOKENS // BLOCK, D), jnp.float32, -2.0, 2.0)
    offsets = jnp.repeat(offsets, BLOCK, axis=0)
    noise = jnp.clip(jax.random.normal(noise_key, (TOKENS, D), jnp.float32), -6.0, 6.0)
    drawn = noise + offsets
    return drawn.astype(jnp.bfloat16)


def draw_exponent(key, part):
    return exponent_draw(key)


def setup_inputs(seed: int = 0) -> dict:
    splits = jax.random.split(jax.random.key(seed), 5)
    return {
        "query": draw_query(jax.random.fold_in(splits[4], 71), 0),
        "key": draw_key(jax.random.fold_in(splits[4], 71), 0),
        "value": draw_value(jax.random.fold_in(splits[4], 71), 0),
        "exponent": draw_exponent(jax.random.fold_in(splits[4], 71), 0),
    }


def reference(query, key, value, exponent):
    slopes = jnp.exp2(-12.0 * exponent.astype(jnp.float32) / HEADS)
    bands = MIN_BAND + ((exponent.astype(jnp.int32) - 1) * (MAX_BAND - MIN_BAND)) // (HEADS - 1)
    query_rows = min(512, TOKENS)
    window_rows = MAX_BAND * BLOCK
    factor = HS ** -0.5
    heads_query = query.reshape(TOKENS, HEADS, HS).transpose(1, 0, 2)
    padding = jnp.zeros((HEADS, window_rows, HS), key.dtype)
    heads_key = jnp.concatenate([padding, key.reshape(TOKENS, HEADS, HS).transpose(1, 0, 2)], axis=1)
    heads_value = jnp.concatenate([padding, value.reshape(TOKENS, HEADS, HS).transpose(1, 0, 2)], axis=1)

    def one_head(packed):
        query_head, key_head, value_head, head_slope, head_band = packed

        def one_block(block_id):
            first = (block_id * query_rows).astype(jnp.int32)
            query_block = lax.dynamic_slice_in_dim(query_head, first, query_rows, 0)
            key_window = lax.dynamic_slice_in_dim(key_head, first, window_rows + query_rows, 0)
            value_window = lax.dynamic_slice_in_dim(value_head, first, window_rows + query_rows, 0)
            query_pos = first + jnp.arange(query_rows, dtype=jnp.int32)
            key_pos = first - window_rows + jnp.arange(window_rows + query_rows, dtype=jnp.int32)
            distance = query_pos[:, None] - key_pos[None, :]
            scores = jnp.dot(query_block, key_window.T, preferred_element_type=jnp.float32) * factor
            scores = scores - head_slope * distance.astype(jnp.float32)
            live = (key_pos[None, :] >= 0) & (distance >= 0) & (query_pos[:, None] // BLOCK - key_pos[None, :] // BLOCK < head_band)
            scores = jnp.where(live, scores, -1.0e30)
            highest = jnp.max(scores, axis=1, keepdims=True)
            weights = jnp.where(live, jnp.exp(scores - highest), 0.0)
            weight_sum = jnp.sum(weights, axis=1, keepdims=True)
            mixed = jnp.dot(weights.astype(jnp.bfloat16), value_window, preferred_element_type=jnp.float32)
            return (mixed / weight_sum).astype(jnp.bfloat16)

        blocks = lax.map(one_block, jnp.arange(TOKENS // query_rows, dtype=jnp.int32))
        return blocks.reshape(TOKENS, HS)

    result = lax.map(one_head, (heads_query, heads_key, heads_value, slopes, bands))
    return result.transpose(1, 0, 2).reshape(TOKENS, D)
```

```python
import functools
import math

import jax
import jax.numpy as jnp
from jax import lax
from jax.experimental import pallas as pl
from jax.experimental.pallas import tpu as pltpu
from jax.sharding import PartitionSpec as P

BLOCK = 128
MIN_BAND = 16
MAX_BAND = 40
AXES = ("seq", "head")
LANES = 128
DEAD = -1e30
LOG2E = 1.4426950408889634


def turn_in_kernel(q_ref, k_ref, v_ref, out_ref):
    heads, _, width, rows = out_ref.shape
    for which, ref in enumerate((q_ref, k_ref, v_ref)):
        turned = ref[...].T
        for head in range(heads):
            out_ref[head, which] = turned[head * width : (head + 1) * width]


def turn_in(query, key, value, first, heads, width):
    rows = query.shape[0]
    step = LANES // math.gcd(width, LANES)
    start = first // step
    spec = pl.BlockSpec((rows, step * width), lambda i: (0, i + start))
    return pl.pallas_call(
        turn_in_kernel,
        grid=(heads // step,),
        in_specs=[spec] * 3,
        out_specs=pl.BlockSpec((step, 3, width, rows), lambda i: (i, 0, 0, 0)),
        out_shape=jax.ShapeDtypeStruct((heads, 3, width, rows), query.dtype),
        cost_estimate=pl.CostEstimate(
            flops=0, transcendentals=0, bytes_accessed=12 * heads * width * rows
        ),
        name="turn_in",
    )(query, key, value)


def turn_out_kernel(in_ref, out_ref):
    heads, width, rows = in_ref.shape
    out_ref[...] = in_ref[...].reshape(heads * width, rows).T


def turn_out(parts):
    heads, width, rows = parts.shape
    step = LANES // math.gcd(width, LANES)
    return pl.pallas_call(
        turn_out_kernel,
        grid=(heads // step,),
        in_specs=[pl.BlockSpec((step, width, rows), lambda i: (i, 0, 0))],
        out_specs=pl.BlockSpec((rows, step * width), lambda i: (0, i)),
        out_shape=jax.ShapeDtypeStruct((rows, heads * width), parts.dtype),
        cost_estimate=pl.CostEstimate(
            flops=0, transcendentals=0, bytes_accessed=4 * heads * width * rows
        ),
        name="turn_out",
    )(parts)


def attend_kernel(heads_total, slope_ref, band_ref, qkv_ref, out_ref, keys, values):
    blocks, _, width, rows = qkv_ref.shape
    pad = LANES - width
    tile = 2 * rows
    factor = LOG2E * width**-0.5
    slope = slope_ref[0]
    band = band_ref[0]

    row16 = lax.broadcasted_iota(jnp.int32, (pad, rows), 0)
    lane = lax.broadcasted_iota(jnp.int32, (pad, rows), 1)

    def fill(block, carry):
        at = pl.multiple_of(block * rows, rows)
        bias = (slope * (width**0.5)) * (at + lane).astype(jnp.float32)
        high = bias.astype(jnp.bfloat16).astype(jnp.float32)
        rest = bias - high
        middle = rest.astype(jnp.bfloat16).astype(jnp.float32)
        low = rest - middle
        extra = jnp.where(
            row16 == 0, high, jnp.where(row16 == 1, middle, jnp.where(row16 == 2, low, 0.0))
        ).astype(jnp.bfloat16)
        keys[pl.ds(at, rows), :] = jnp.concatenate([qkv_ref[block, 1], extra], axis=0).T
        values[:width, pl.ds(at, rows)] = qkv_ref[block, 2]
        values[width:, pl.ds(at, rows)] = jnp.ones((pad, rows), jnp.bfloat16)
        return carry

    lax.fori_loop(0, blocks, fill, 0)

    ones = jnp.ones((pad, tile), jnp.bfloat16)

    def attend_tile(index, carry):
        first = 2 * index
        query = jnp.concatenate([qkv_ref[first, 0], qkv_ref[first + 1, 0]], axis=1)
        query = jnp.concatenate([query, ones], axis=0)

        def scores(start, count):
            return jnp.dot(
                keys[pl.ds(start, count), :], query, preferred_element_type=jnp.float32
            )

        def weighed(weights, start, count):
            return jnp.dot(
                values[:, pl.ds(start, count)],
                weights.astype(jnp.bfloat16),
                preferred_element_type=jnp.float32,
            )

        def step(start, count, live, state):
            top, total = state
            score = scores(start, count)
            if live is not None:
                score = jnp.where(live(start, count), score, DEAD)
            new_top = jnp.maximum(top, jnp.max(score, axis=0, keepdims=True))
            weights = jnp.exp2(score * factor - new_top * factor)
            shrink = jnp.exp2((top - new_top) * factor)
            return new_top, total * shrink + weighed(weights, start, count)

        def live(start, count):
            key_pos = start + lax.broadcasted_iota(jnp.int32, (count, tile), 0)
            query_pos = first * rows + lax.broadcasted_iota(jnp.int32, (count, tile), 1)
            return (query_pos >= key_pos) & (query_pos // BLOCK - key_pos // BLOCK < band)

        state = (
            jnp.full((1, tile), DEAD, jnp.float32),
            jnp.zeros((LANES, tile), jnp.float32),
        )
        state = step(pl.multiple_of(first * rows, tile), tile, live, state)
        pairs = jnp.minimum(first, band - 2) // 2
        quads = pairs // 2
        edge = jnp.where(first > 2 * pairs, 1, 0)

        def quad_step(j, state):
            start = pl.multiple_of((first - 4 * (j + 1)) * rows, tile)
            return step(start, 2 * tile, None, state)

        state = lax.fori_loop(0, quads, quad_step, state)

        def pair_step(j, state):
            start = pl.multiple_of((first - 4 * quads - 2 * (j + 1)) * rows, tile)
            return step(start, tile, live, state)

        state = lax.fori_loop(0, pairs - 2 * quads + edge, pair_step, state)
        total = state[1]
        result = (total[:width] / total[width : width + 1]).astype(jnp.bfloat16)
        out_ref[first] = result[:, :rows]
        out_ref[first + 1] = result[:, rows:]
        return carry

    lax.fori_loop(0, blocks // 2, attend_tile, 0)


def attend(qkv, slope, band, heads_total):
    blocks, _, width, rows = qkv.shape
    pairs = blocks * (blocks + 1) // 2
    return pl.pallas_call(
        functools.partial(attend_kernel, heads_total),
        in_specs=[
            pl.BlockSpec(memory_space=pltpu.SMEM),
            pl.BlockSpec(memory_space=pltpu.SMEM),
            pl.BlockSpec(memory_space=pltpu.VMEM),
        ],
        out_specs=pl.BlockSpec(memory_space=pltpu.VMEM),
        out_shape=jax.ShapeDtypeStruct((blocks, width, rows), jnp.bfloat16),
        scratch_shapes=[
            pltpu.VMEM((blocks * rows, LANES), jnp.bfloat16),
            pltpu.VMEM((LANES, blocks * rows), jnp.bfloat16),
        ],
        compiler_params=pltpu.CompilerParams(vmem_limit_bytes=40 * 2**20),
        cost_estimate=pl.CostEstimate(
            flops=4 * pairs * rows * rows * LANES,
            transcendentals=pairs * rows * rows,
            bytes_accessed=8 * blocks * width * rows,
        ),
        name="attend",
    )(slope, band, qkv)


def on_device(query, key, value, exponent):
    rows, width_total = query.shape
    heads = exponent.shape[0]
    width = width_total // heads
    devices = lax.axis_size("seq") * lax.axis_size("head")
    me = lax.axis_index("seq") * lax.axis_size("head") + lax.axis_index("head")
    share = max(1, devices // heads)
    owners = devices // share
    rounds = heads // owners

    band = MIN_BAND + (exponent - 1) * (MAX_BAND - MIN_BAND) // (heads - 1)
    slope = jnp.exp2(-12.0 * exponent.astype(jnp.float32) / heads)

    outs = []
    for part in range(rounds):
        sent = turn_in(query, key, value, part * owners, owners, width)
        if share > 1:
            sent = jnp.repeat(sent, share, axis=0)
        qkv = lax.all_to_all(sent, AXES, 0, 0, tiled=True)
        head = part * owners + me // share
        mine = lax.dynamic_slice_in_dim(slope, head, 1), lax.dynamic_slice_in_dim(band, head, 1)
        result = attend(qkv, *mine, heads)
        back = lax.all_to_all(result, AXES, 0, 0, tiled=True)
        if share > 1:
            back = back.reshape(owners, share, width, rows)[:, 0]
        outs.append(turn_out(back))
    return jnp.concatenate(outs, axis=1)


def solution(mesh):
    spec = P(AXES, None)
    return jax.shard_map(
        on_device,
        mesh=mesh,
        in_specs=(spec, spec, spec, P()),
        out_specs=spec,
        check_vma=False,
    )
```

```python
import functools
import math

import jax
import jax.numpy as jnp
from jax import lax
from jax.experimental import pallas as pl
from jax.experimental.pallas import tpu as pltpu
from jax.sharding import PartitionSpec as P

BLOCK = 128
MIN_BAND = 16
MAX_BAND = 40
AXES = ("seq", "head")
LANES = 128
DEAD = -1e30
LOG2E = 1.4426950408889634
PIECE = 256
SPAN = 100.0


def turn_in_kernel(q_ref, k_ref, v_ref, out_ref):
    heads, _, width, rows = out_ref.shape
    for which, ref in enumerate((q_ref, k_ref, v_ref)):
        turned = ref[...].T
        for head in range(heads):
            out_ref[head, which] = turned[head * width : (head + 1) * width]


def turn_in(query, key, value, first, heads, width):
    rows = query.shape[0]
    step = LANES // math.gcd(width, LANES)
    start = first // step
    spec = pl.BlockSpec((rows, step * width), lambda i: (0, i + start))
    return pl.pallas_call(
        turn_in_kernel,
        grid=(heads // step,),
        in_specs=[spec] * 3,
        out_specs=pl.BlockSpec((step, 3, width, rows), lambda i: (i, 0, 0, 0)),
        out_shape=jax.ShapeDtypeStruct((heads, 3, width, rows), query.dtype),
        cost_estimate=pl.CostEstimate(
            flops=0, transcendentals=0, bytes_accessed=12 * heads * width * rows
        ),
        name="turn_in",
    )(query, key, value)


def turn_out_kernel(in_ref, *refs):
    heads, width, rows = in_ref.shape
    refs[-1][...] = in_ref[...].reshape(heads * width, rows).T


def turn_out(parts, first, so_far, heads_total):
    heads, width, rows = parts.shape
    step = LANES // math.gcd(width, LANES)
    start = first // step
    given = () if so_far is None else (so_far,)
    return pl.pallas_call(
        turn_out_kernel,
        grid=(heads // step,),
        in_specs=[pl.BlockSpec((step, width, rows), lambda i: (i, 0, 0))]
        + [pl.BlockSpec(memory_space=pl.ANY)] * len(given),
        out_specs=pl.BlockSpec((rows, step * width), lambda i: (0, i + start)),
        out_shape=jax.ShapeDtypeStruct((rows, heads_total * width), parts.dtype),
        input_output_aliases={1: 0} if given else {},
        cost_estimate=pl.CostEstimate(
            flops=0, transcendentals=0, bytes_accessed=4 * heads * width * rows
        ),
        name="turn_out",
    )(parts, *given)


def attend_kernel(sub, slope_ref, band_ref, qkv_ref, out_ref, keys, values):
    blocks, _, width, rows = qkv_ref.shape
    pad = LANES - width
    half = 2 * rows
    per = 2 * sub
    factor = LOG2E * width**-0.5
    slope = slope_ref[0]
    band = band_ref[0]

    row = lax.broadcasted_iota(jnp.int32, (pad, rows), 0)
    lane = lax.broadcasted_iota(jnp.int32, (pad, rows), 1)

    def fill(block, carry):
        at = pl.multiple_of(block * rows, rows)
        bias = (slope * width**0.5) * (at + lane).astype(jnp.float32)
        high = bias.astype(jnp.bfloat16).astype(jnp.float32)
        rest = bias - high
        middle = rest.astype(jnp.bfloat16).astype(jnp.float32)
        low = rest - middle
        extra = jnp.where(
            row == 0, high, jnp.where(row == 1, middle, jnp.where(row == 2, low, 0.0))
        ).astype(jnp.bfloat16)
        keys[pl.ds(at, rows), :] = jnp.concatenate([qkv_ref[block, 1], extra], axis=0).T
        values[:width, pl.ds(at, rows)] = qkv_ref[block, 2]
        values[width:, pl.ds(at, rows)] = jnp.ones((pad, rows), jnp.bfloat16)
        return carry

    lax.fori_loop(0, blocks, fill, 0, unroll=4)
    ones = jnp.ones((pad, half), jnp.bfloat16)

    def attend_tile(index, carry):
        first = per * index

        def query_of(s):
            pair = [qkv_ref[first + 2 * s, 0], qkv_ref[first + 2 * s + 1, 0]]
            return jnp.concatenate([jnp.concatenate(pair, axis=1), ones], axis=0)

        def live(start, count, s):
            key_pos = start + lax.broadcasted_iota(jnp.int32, (count, half), 0)
            query_pos = (first + 2 * s) * rows + lax.broadcasted_iota(jnp.int32, (count, half), 1)
            return (query_pos >= key_pos) & (query_pos // BLOCK - key_pos // BLOCK < band)

        def scored(start, count, s, masked, query):
            score = jnp.dot(keys[pl.ds(start, count), :], query, preferred_element_type=jnp.float32)
            return jnp.where(live(start, count, s), score, DEAD) if masked else score

        def weighed(start, count, weights):
            return jnp.dot(
                values[:, pl.ds(start, count)],
                weights.astype(jnp.bfloat16),
                preferred_element_type=jnp.float32,
            )

        def slow_step(start, count, s, masked, query, state):
            top, total = state
            score = scored(start, count, s, masked, query)
            new_top = jnp.maximum(top, jnp.max(score, axis=0, keepdims=True))
            weights = jnp.exp2(score * factor - new_top * factor)
            shrink = jnp.exp2((top - new_top) * factor)
            return new_top, total * shrink + weighed(start, count, weights)

        def fast_step(start, count, s, masked, query, state):
            top, total, high = state
            pieces = []
            for at in range(0, count, PIECE):
                score = scored(start + at, PIECE, s, masked, query)
                pieces.append(jnp.exp2(score * factor - top * factor).astype(jnp.bfloat16))
                high = jnp.maximum(high, jnp.max(score.reshape(PIECE // 8, 8, half), axis=0))
            return top, total + weighed(start, count, jnp.concatenate(pieces, axis=0)), high

        whole = jnp.minimum(first, band - per) // per
        needed = jnp.minimum(first, band - 1)
        rest = (needed - per * whole + per - 1) // per

        def sweep(step, queries, states):
            def steps(masked):
                def body(j, states):
                    start = pl.multiple_of((first - per * (j + 1)) * rows, half)
                    return [
                        step(start, per * rows, s, masked, queries[s], states[s])
                        for s in range(sub)
                    ]

                return body

            states = lax.fori_loop(0, whole, steps(False), states)
            return lax.fori_loop(whole, whole + rest, steps(True), states)

        def finish(s, total):
            result = (total[:width] / total[width : width + 1]).astype(jnp.bfloat16)
            out_ref[first + 2 * s] = result[:, :rows]
            out_ref[first + 2 * s + 1] = result[:, rows:]

        queries = [query_of(s) for s in range(sub)]
        states = []
        for s in range(sub):
            start = pl.multiple_of((first + 2 * s) * rows, half)
            score = scored(start, half, s, True, queries[s])
            top = jnp.max(score, axis=0, keepdims=True)
            total = weighed(start, half, jnp.exp2(score * factor - top * factor))
            state = (top, total, jnp.full((8, half), DEAD, jnp.float32))
            if s:
                start = pl.multiple_of(first * rows, half)
                state = fast_step(start, half * s, s, False, queries[s], state)
            states.append(state)
        states = sweep(fast_step, queries, states)
        worst = jnp.float32(DEAD)
        for s in range(sub):
            top, total, high = states[s]
            finish(s, total)
            worst = jnp.maximum(worst, jnp.max(high - top))

        @pl.when(worst * factor > SPAN)
        def _():
            queries = [query_of(s) for s in range(sub)]
            states = []
            for s in range(sub):
                state = (
                    jnp.full((1, half), DEAD, jnp.float32),
                    jnp.zeros((LANES, half), jnp.float32),
                )
                start = pl.multiple_of(first * rows, half)
                states.append(slow_step(start, half * (s + 1), s, True, queries[s], state))
            states = sweep(slow_step, queries, states)
            for s in range(sub):
                finish(s, states[s][1])

        return carry

    lax.fori_loop(0, blocks // per, attend_tile, 0)


def attend(qkv, slope, band, heads_total):
    blocks, _, width, rows = qkv.shape
    pairs = blocks * (blocks + 1) // 2
    sub = math.gcd(blocks, 8) // 2
    return pl.pallas_call(
        functools.partial(attend_kernel, sub),
        in_specs=[
            pl.BlockSpec(memory_space=pltpu.SMEM),
            pl.BlockSpec(memory_space=pltpu.SMEM),
            pl.BlockSpec(memory_space=pltpu.VMEM),
        ],
        out_specs=pl.BlockSpec(memory_space=pltpu.VMEM),
        out_shape=jax.ShapeDtypeStruct((blocks, width, rows), jnp.bfloat16),
        scratch_shapes=[
            pltpu.VMEM((blocks * rows, LANES), jnp.bfloat16),
            pltpu.VMEM((LANES, blocks * rows), jnp.bfloat16),
        ],
        compiler_params=pltpu.CompilerParams(vmem_limit_bytes=32 * 2**20),
        cost_estimate=pl.CostEstimate(
            flops=4 * pairs * rows * rows * LANES,
            transcendentals=pairs * rows * rows,
            bytes_accessed=8 * blocks * width * rows,
        ),
        name="attend",
    )(slope, band, qkv)


def on_device(query, key, value, exponent):
    rows, width_total = query.shape
    heads = exponent.shape[0]
    width = width_total // heads
    devices = lax.axis_size("seq") * lax.axis_size("head")
    me = lax.axis_index("seq") * lax.axis_size("head") + lax.axis_index("head")
    share = max(1, devices // heads)
    owners = devices // share
    rounds = heads // owners

    band = MIN_BAND + (exponent - 1) * (MAX_BAND - MIN_BAND) // (heads - 1)
    slope = jnp.exp2(-12.0 * exponent.astype(jnp.float32) / heads)

    out = None
    for part in range(rounds):
        sent = turn_in(query, key, value, part * owners, owners, width)
        if share > 1:
            sent = jnp.repeat(sent, share, axis=0)
        qkv = lax.all_to_all(sent, AXES, 0, 0, tiled=True)
        head = part * owners + me // share
        mine = lax.dynamic_slice_in_dim(slope, head, 1), lax.dynamic_slice_in_dim(band, head, 1)
        result = attend(qkv, *mine, heads)
        back = lax.all_to_all(result, AXES, 0, 0, tiled=True)
        if share > 1:
            back = back.reshape(owners, share, width, rows)[:, 0]
        out = turn_out(back, part * owners, out, heads)
    return out


def solution(mesh):
    spec = P(AXES, None)
    return jax.shard_map(
        on_device,
        mesh=mesh,
        in_specs=(spec, spec, spec, P()),
        out_specs=spec,
        check_vma=False,
    )
```

```python
import functools
import math

import jax
import jax.numpy as jnp
from jax import lax
from jax.experimental import pallas as pl
from jax.experimental.pallas import tpu as pltpu
from jax.sharding import PartitionSpec as P

BLOCK = 128
MIN_BAND = 16
MAX_BAND = 40
AXES = ("seq", "head")
LANES = 128
DEAD = -1e30
LOG2E = 1.4426950408889634
PIECE = 256
SPAN = 100.0
LOTS = 4


def turn_in_kernel(q_ref, k_ref, v_ref, out_ref):
    heads, _, width, rows = out_ref.shape
    for which, ref in enumerate((q_ref, k_ref, v_ref)):
        turned = ref[...].T
        for head in range(heads):
            out_ref[head, which] = turned[head * width : (head + 1) * width]


def turn_in(query, key, value, first, heads, width):
    rows = query.shape[0]
    step = math.gcd(heads, 2 * LANES // math.gcd(width, LANES))
    start = first // step
    spec = pl.BlockSpec((rows, step * width), lambda i: (0, i + start))
    return pl.pallas_call(
        turn_in_kernel,
        grid=(heads // step,),
        in_specs=[spec] * 3,
        out_specs=pl.BlockSpec((step, 3, width, rows), lambda i: (i, 0, 0, 0)),
        out_shape=jax.ShapeDtypeStruct((heads, 3, width, rows), query.dtype),
        cost_estimate=pl.CostEstimate(
            flops=0, transcendentals=0, bytes_accessed=12 * heads * width * rows
        ),
        name="turn_in",
    )(query, key, value)


def turn_out_kernel(first, in_ref, *refs):
    out_ref, turned, sems = refs[-3:]
    heads, width, rows = in_ref.shape
    lots, _, span = turned.shape
    some = heads // lots
    copies = []
    for i in range(lots):
        turned[i] = in_ref[i * some : (i + 1) * some].reshape(span, rows).T
        columns = pl.ds(first * width + i * span, span)
        copies.append(pltpu.make_async_copy(turned.at[i], out_ref.at[:, columns], sems.at[i]))
        copies[-1].start()
    for copy in copies:
        copy.wait()


def turn_out(parts, first, so_far, heads_total):
    heads, width, rows = parts.shape
    lots = math.gcd(LOTS, heads * width // LANES)
    given = () if so_far is None else (so_far,)
    return pl.pallas_call(
        functools.partial(turn_out_kernel, first),
        in_specs=[pl.BlockSpec(memory_space=pltpu.VMEM)]
        + [pl.BlockSpec(memory_space=pl.ANY)] * len(given),
        out_specs=pl.BlockSpec(memory_space=pl.ANY),
        out_shape=jax.ShapeDtypeStruct((rows, heads_total * width), parts.dtype),
        input_output_aliases={1: 0} if given else {},
        scratch_shapes=[
            pltpu.VMEM((lots, rows, heads * width // lots), parts.dtype),
            pltpu.SemaphoreType.DMA((lots,)),
        ],
        cost_estimate=pl.CostEstimate(
            flops=0, transcendentals=0, bytes_accessed=4 * heads * width * rows
        ),
        name="turn_out",
    )(parts, *given)


def attend_kernel(sub, v_parts, parts_out, slope_ref, band_ref, given_ref, *refs):
    v_refs, out_refs, refs = refs[:v_parts], refs[v_parts : v_parts + parts_out], refs[v_parts + parts_out :]
    keys, values, refs = refs[0], refs[1], refs[2:]
    blocks, _, width, rows = given_ref.shape
    staged = refs if parts_out > 1 else ()
    qkv_ref = staged[0] if staged else given_ref
    out_ref = refs[-1] if parts_out > 1 else out_refs[0]
    seq, slot = lax.axis_index("seq"), lax.axis_index("head")
    slots = lax.axis_size("head")
    pad = LANES - width
    half = 2 * rows
    per = 2 * sub
    factor = LOG2E * width**-0.5
    slope = slope_ref[0]
    band = band_ref[0]

    row = lax.broadcasted_iota(jnp.int32, (pad, rows), 0)
    lane = lax.broadcasted_iota(jnp.int32, (pad, rows), 1)

    def fill(block, carry):
        at = pl.multiple_of(block * rows, rows)
        bias = (slope * width**0.5) * (at + lane).astype(jnp.float32)
        high = bias.astype(jnp.bfloat16).astype(jnp.float32)
        rest = bias - high
        middle = rest.astype(jnp.bfloat16).astype(jnp.float32)
        low = rest - middle
        extra = jnp.where(
            row == 0, high, jnp.where(row == 1, middle, jnp.where(row == 2, low, 0.0))
        ).astype(jnp.bfloat16)
        keys[pl.ds(at, rows), :] = jnp.concatenate([qkv_ref[block, 1], extra], axis=0).T
        if not v_parts:
            values[:width, pl.ds(at, rows)] = qkv_ref[block, 2]
        values[width:, pl.ds(at, rows)] = jnp.ones((pad, rows), jnp.bfloat16)
        return carry

    if staged:
        lot = blocks // LOTS
        copies = []
        for i in range(LOTS):
            some = pl.ds(i * lot, lot)
            copies.append(
                pltpu.make_async_copy(given_ref.at[some], qkv_ref.at[some], staged[1].at[i])
            )
            copies[-1].start()
        for i in range(LOTS):
            copies[i].wait()
            lax.fori_loop(i * lot, (i + 1) * lot, fill, 0, unroll=4)
    else:
        lax.fori_loop(0, blocks, fill, 0, unroll=4)
    for flip, ref in enumerate(v_refs):
        for shift in range(slots):
            block = (seq ^ flip) * slots + (slot + slots - shift) % slots
            at = pl.multiple_of(block * rows, rows)
            values[:width, pl.ds(at, rows)] = ref[shift]
    ones = jnp.ones((pad, half), jnp.bfloat16)

    def attend_tile(index, carry):
        first = per * index

        def query_of(s):
            pair = [qkv_ref[first + 2 * s, 0], qkv_ref[first + 2 * s + 1, 0]]
            return jnp.concatenate([jnp.concatenate(pair, axis=1), ones], axis=0)

        def live(start, count, s):
            key_pos = start + lax.broadcasted_iota(jnp.int32, (count, half), 0)
            query_pos = (first + 2 * s) * rows + lax.broadcasted_iota(jnp.int32, (count, half), 1)
            return (query_pos >= key_pos) & (query_pos // BLOCK - key_pos // BLOCK < band)

        def scored(start, count, s, masked, query):
            score = jnp.dot(keys[pl.ds(start, count), :], query, preferred_element_type=jnp.float32)
            return jnp.where(live(start, count, s), score, DEAD) if masked else score

        def weighed(start, count, weights):
            return jnp.dot(
                values[:, pl.ds(start, count)],
                weights.astype(jnp.bfloat16),
                preferred_element_type=jnp.float32,
            )

        def slow_step(start, count, s, masked, query, state):
            top, total = state
            score = scored(start, count, s, masked, query)
            new_top = jnp.maximum(top, jnp.max(score, axis=0, keepdims=True))
            weights = jnp.exp2(score * factor - new_top * factor)
            shrink = jnp.exp2((top - new_top) * factor)
            return new_top, total * shrink + weighed(start, count, weights)

        def fast_step(start, count, s, masked, query, state):
            top, total, high = state
            pieces = []
            for at in range(0, count, PIECE):
                score = scored(start + at, PIECE, s, masked, query)
                pieces.append(jnp.exp2(score * factor - top * factor).astype(jnp.bfloat16))
                high = jnp.maximum(high, jnp.max(score.reshape(PIECE // 8, 8, half), axis=0))
            return top, total + weighed(start, count, jnp.concatenate(pieces, axis=0)), high

        whole = jnp.minimum(first, band - per) // per
        needed = jnp.minimum(first, band - 1)
        rest = (needed - per * whole + per - 1) // per

        def sweep(step, queries, states):
            def steps(masked):
                def body(j, states):
                    start = pl.multiple_of((first - per * (j + 1)) * rows, half)
                    return [
                        step(start, per * rows, s, masked, queries[s], states[s])
                        for s in range(sub)
                    ]

                return body

            states = lax.fori_loop(0, whole, steps(False), states)
            return lax.fori_loop(whole, whole + rest, steps(True), states)

        def finish(s, total):
            result = (total[:width] / total[width : width + 1]).astype(jnp.bfloat16)
            out_ref[first + 2 * s] = result[:, :rows]
            out_ref[first + 2 * s + 1] = result[:, rows:]

        queries = [query_of(s) for s in range(sub)]
        states = []
        for s in range(sub):
            start = pl.multiple_of((first + 2 * s) * rows, half)
            score = scored(start, half, s, True, queries[s])
            top = jnp.max(score, axis=0, keepdims=True)
            total = weighed(start, half, jnp.exp2(score * factor - top * factor))
            state = (top, total, jnp.full((8, half), DEAD, jnp.float32))
            if s:
                start = pl.multiple_of(first * rows, half)
                state = fast_step(start, half * s, s, False, queries[s], state)
            states.append(state)
        states = sweep(fast_step, queries, states)
        worst = jnp.float32(DEAD)
        for s in range(sub):
            top, total, high = states[s]
            finish(s, total)
            worst = jnp.maximum(worst, jnp.max(high - top))

        @pl.when(worst * factor > SPAN)
        def _():
            queries = [query_of(s) for s in range(sub)]
            states = []
            for s in range(sub):
                state = (
                    jnp.full((1, half), DEAD, jnp.float32),
                    jnp.zeros((LANES, half), jnp.float32),
                )
                start = pl.multiple_of(first * rows, half)
                states.append(slow_step(start, half * (s + 1), s, True, queries[s], state))
            states = sweep(slow_step, queries, states)
            for s in range(sub):
                finish(s, states[s][1])

        return carry

    lax.fori_loop(0, blocks // per, attend_tile, 0)
    if parts_out > 1:
        for flip, ref in enumerate(out_refs):
            ref[...] = out_ref[pl.ds((seq ^ flip) * slots, slots)]


def attend(given, slope, band, values=(), parts_out=1):
    blocks, _, width, rows = given.shape
    pairs = blocks * (blocks + 1) // 2
    sub = math.gcd(blocks, 8) // 2
    shape = (blocks // parts_out, width, rows)
    staged = [pltpu.VMEM(given.shape, given.dtype), pltpu.SemaphoreType.DMA((LOTS,))]
    results = pl.pallas_call(
        functools.partial(attend_kernel, sub, len(values), parts_out),
        in_specs=[
            pl.BlockSpec(memory_space=pltpu.SMEM),
            pl.BlockSpec(memory_space=pltpu.SMEM),
            pl.BlockSpec(memory_space=pltpu.VMEM if parts_out == 1 else pl.ANY),
        ]
        + [pl.BlockSpec(memory_space=pltpu.VMEM)] * len(values),
        out_specs=[pl.BlockSpec(memory_space=pltpu.VMEM)] * parts_out,
        out_shape=[jax.ShapeDtypeStruct(shape, given.dtype)] * parts_out,
        scratch_shapes=[
            pltpu.VMEM((blocks * rows, LANES), given.dtype),
            pltpu.VMEM((LANES, blocks * rows), given.dtype),
        ]
        + (staged if parts_out > 1 else [])
        + ([pltpu.VMEM((blocks, width, rows), given.dtype)] if parts_out > 1 else []),
        compiler_params=pltpu.CompilerParams(vmem_limit_bytes=28 * 2**20),
        cost_estimate=pl.CostEstimate(
            flops=4 * pairs * rows * rows * LANES,
            transcendentals=pairs * rows * rows,
            bytes_accessed=8 * blocks * width * rows,
        ),
        name="attend",
    )(slope, band, given, *values)
    return results if parts_out > 1 else results[0]


def after(value, *others):
    return lax.optimization_barrier((value, *others))[0]


def moved(shapes, dtype, name, kernel, operands, scratch=(), where=None):
    specs = where or [pl.BlockSpec(memory_space=pltpu.VMEM)] * len(operands)
    size = 4 * sum(math.prod(shape) for shape in shapes)
    return pl.pallas_call(
        kernel,
        in_specs=specs,
        out_specs=[pl.BlockSpec(memory_space=pltpu.VMEM)] * len(shapes),
        out_shape=[jax.ShapeDtypeStruct(shape, dtype) for shape in shapes],
        scratch_shapes=list(scratch),
        cost_estimate=pl.CostEstimate(flops=0, transcendentals=0, bytes_accessed=size),
        name=name,
    )(*operands)


def cut_kernel(first, value_ref, *refs):
    outs, sems = refs[:-1], refs[-1]
    slot, slots = lax.axis_index("head"), lax.axis_size("head")
    span = outs[0].shape[1]
    copies = []
    for i, out in enumerate(outs):
        column = pl.multiple_of(first + ((slot + i + 1) % slots) * span, LANES)
        copies.append(pltpu.make_async_copy(value_ref.at[:, pl.ds(column, span)], out, sems.at[i]))
        copies[-1].start()
    for copy in copies:
        copy.wait()


def cut(value, first, span):
    slots = lax.axis_size("head")
    return moved(
        [(value.shape[0], span)] * (slots - 1),
        value.dtype,
        "cut",
        functools.partial(cut_kernel, first),
        [value],
        [pltpu.SemaphoreType.DMA((slots - 1,))],
        [pl.BlockSpec(memory_space=pl.ANY)],
    )


def turn_values_kernel(first, value_ref, *refs):
    slot, slots = lax.axis_index("head"), lax.axis_size("head")
    came, outs = refs[: slots - 1], refs[slots - 1 : -3]
    own, turned, sem = refs[-3:]
    span = own.shape[1]
    width = outs[0].shape[1]
    seq = lax.axis_index("seq")
    column = pl.multiple_of(first + slot * span, LANES)
    copy = pltpu.make_async_copy(value_ref.at[:, pl.ds(column, span)], own, sem)
    copy.start()
    for shift in [*range(1, slots), 0]:
        if shift == 0:
            copy.wait()
        turned[...] = (own if shift == 0 else came[shift - 1])[...].T
        for flip, out in enumerate(outs):
            at = pl.multiple_of((seq ^ flip) * width, 16)
            out[shift] = turned[pl.ds(at, width), :]


def turn_values(value, came, first, width):
    seqs, slots = lax.axis_size("seq"), lax.axis_size("head")
    rows, span = came[0].shape
    return moved(
        [(slots, width, rows)] * seqs,
        value.dtype,
        "turn_values",
        functools.partial(turn_values_kernel, first),
        [value, *came],
        [
            pltpu.VMEM((rows, span), value.dtype),
            pltpu.VMEM((span, rows), value.dtype),
            pltpu.SemaphoreType.DMA(()),
        ],
        [pl.BlockSpec(memory_space=pl.ANY)] + [pl.BlockSpec(memory_space=pltpu.VMEM)] * len(came),
    )


def regroup_kernel(*refs):
    seq, slot = lax.axis_index("seq"), lax.axis_index("head")
    seqs, slots = lax.axis_size("seq"), lax.axis_size("head")
    for flip in range(seqs):
        for shift in range(slots):
            refs[seqs + shift][seq ^ flip] = refs[flip][(slot + shift) % slots]


def regroup(came):
    seqs, slots = lax.axis_size("seq"), lax.axis_size("head")
    shape = (seqs, *came[0].shape[1:])
    return moved([shape] * slots, came[0].dtype, "regroup", regroup_kernel, came)


def turn_in_slots_kernel(arrays, *refs):
    out_ref = refs[-1]
    seqs, slots, _, width, rows = out_ref.shape
    for which in range(arrays):
        turned = refs[which][...].T
        for slot in range(slots):
            for seq in range(seqs):
                at = (slot * seqs + seq) * width
                out_ref[seq, slot, which] = turned[at : at + width]


def turn_in_slots(arrays, first, width):
    seqs, slots = lax.axis_size("seq"), lax.axis_size("head")
    rows = arrays[0].shape[0]
    step = math.gcd(slots, 2)
    start = first // (step * seqs)
    spec = pl.BlockSpec((rows, step * seqs * width), lambda i: (0, i + start))
    count = len(arrays)
    out = pl.pallas_call(
        functools.partial(turn_in_slots_kernel, count),
        grid=(slots // step,),
        in_specs=[spec] * count,
        out_specs=pl.BlockSpec((seqs, step, count, width, rows), lambda i: (0, i, 0, 0, 0)),
        out_shape=jax.ShapeDtypeStruct((seqs, slots, count, width, rows), arrays[0].dtype),
        cost_estimate=pl.CostEstimate(
            flops=0,
            transcendentals=0,
            bytes_accessed=4 * count * seqs * slots * width * rows,
        ),
        name="turn_in_slots",
    )(*arrays)
    return out.reshape(seqs * slots, count, width, rows)


def turn_out_slots_kernel(first, parts, *refs):
    out_ref, turned, sems = refs[-3:]
    slots, rows, span = turned.shape
    slot = lax.axis_index("head")
    copies = []
    for i in range(slots):
        if parts == 1:
            _, width, _ = refs[0].shape
            heads = [refs[0][seq * slots + i] for seq in range(span // width)]
            some, owner = jnp.concatenate(heads, axis=0), i
        else:
            some, owner = refs[i][...].reshape(span, rows), (slot + slots - i) % slots
        turned[i] = some.T
        columns = pl.ds(pl.multiple_of(first + owner * span, LANES), span)
        copies.append(pltpu.make_async_copy(turned.at[i], out_ref.at[:, columns], sems.at[i]))
        copies[-1].start()
    for copy in copies:
        copy.wait()


def turn_out_slots(parts, first, so_far, width_total):
    slots = lax.axis_size("head")
    rows = parts[0].shape[-1]
    span = sum(math.prod(part.shape[:-1]) for part in parts) // slots
    given = () if so_far is None else (so_far,)
    return pl.pallas_call(
        functools.partial(turn_out_slots_kernel, first, len(parts)),
        in_specs=[pl.BlockSpec(memory_space=pltpu.VMEM)] * len(parts)
        + [pl.BlockSpec(memory_space=pl.ANY)] * len(given),
        out_specs=pl.BlockSpec(memory_space=pl.ANY),
        out_shape=jax.ShapeDtypeStruct((rows, width_total), parts[0].dtype),
        input_output_aliases={len(parts): 0} if given else {},
        scratch_shapes=[
            pltpu.VMEM((slots, rows, span), parts[0].dtype),
            pltpu.SemaphoreType.DMA((slots,)),
        ],
        cost_estimate=pl.CostEstimate(
            flops=0, transcendentals=0, bytes_accessed=4 * slots * span * rows
        ),
        name="turn_out_slots",
    )(*parts, *given)


def in_two_sets(query, key, value, slope, band, width):
    seqs, slots = lax.axis_size("seq"), lax.axis_size("head")
    seq, slot = lax.axis_index("seq"), lax.axis_index("head")
    half = seqs * slots
    span = seqs * width

    def send(x, flip, shift):
        to = [
            (s * slots + z, (s ^ flip) * slots + (z + shift) % slots)
            for s in range(seqs)
            for z in range(slots)
        ]
        return x if flip == shift == 0 else lax.ppermute(x, AXES, to)

    def mine(first):
        head = first + slot * seqs + seq
        return [lax.dynamic_slice_in_dim(x, head, 1) for x in (slope, band)]

    raw = (query, key, value)
    given_a = lax.all_to_all(turn_in_slots(raw, 0, width), AXES, 0, 0, tiled=True)
    given_b = lax.all_to_all(turn_in_slots(raw, half, width), AXES, 0, 0, tiled=True)

    result_a = attend(given_a, *mine(0), parts_out=seqs)
    groups = regroup([send(x, flip, 0) for flip, x in enumerate(result_a)])
    *groups, given_b = lax.optimization_barrier((*groups, given_b))
    back_a = [send(x, 0, shift) for shift, x in enumerate(groups)]

    result_b = attend(given_b, *mine(half))
    back_b = lax.all_to_all(after(result_b, *back_a[1:]), AXES, 0, 0, tiled=True)
    out = turn_out_slots(back_a, 0, None, 2 * half * width)
    return turn_out_slots([back_b], half * width, out, 2 * half * width)


def on_device(query, key, value, exponent):
    rows, width_total = query.shape
    heads = exponent.shape[0]
    width = width_total // heads
    seqs, slots = lax.axis_size("seq"), lax.axis_size("head")
    devices = seqs * slots

    band = MIN_BAND + (exponent - 1) * (MAX_BAND - MIN_BAND) // (heads - 1)
    slope = jnp.exp2(-12.0 * exponent.astype(jnp.float32) / heads)

    two_each = heads == 2 * devices and seqs & (seqs - 1) == 0 and slots % 2 == 0
    if two_each and seqs * width % LANES == 0:
        return in_two_sets(query, key, value, slope, band, width)

    me = lax.axis_index("seq") * slots + lax.axis_index("head")
    share = max(1, devices // heads)
    owners = devices // share
    out = None
    for part in range(heads // owners):
        sent = turn_in(query, key, value, part * owners, owners, width)
        if share > 1:
            sent = jnp.repeat(sent, share, axis=0)
        given = lax.all_to_all(sent, AXES, 0, 0, tiled=True)
        head = part * owners + me // share
        mine = [lax.dynamic_slice_in_dim(x, head, 1) for x in (slope, band)]
        result = attend(given, *mine)
        back = lax.all_to_all(result, AXES, 0, 0, tiled=True)
        if share > 1:
            back = back.reshape(owners, share, width, rows)[:, 0]
        out = turn_out(back, part * owners, out, heads)
    return out


def solution(mesh):
    spec = P(AXES, None)
    return jax.shard_map(
        on_device,
        mesh=mesh,
        in_specs=(spec, spec, spec, P()),
        out_specs=spec,
        check_vma=False,
    )
```

```python
import functools
import math

import jax
import jax.numpy as jnp
from jax import lax
from jax.experimental import pallas as pl
from jax.experimental.pallas import tpu as pltpu
from jax.sharding import PartitionSpec as P

BLOCK = 128
MIN_BAND = 16
MAX_BAND = 40
AXES = ("seq", "head")
LANES = 128
DEAD = -1e30
LOG2E = 1.4426950408889634
PIECE = 256
SPAN = 90.0
BESIDE = 400
WHOLE_VMEM = 62 * 2**20
LOTS = 4


def turn_in_kernel(q_ref, k_ref, v_ref, out_ref):
    heads, _, width, rows = out_ref.shape
    for which, ref in enumerate((q_ref, k_ref, v_ref)):
        turned = ref[...].T
        for head in range(heads):
            out_ref[head, which] = turned[head * width : (head + 1) * width]


def turn_in(query, key, value, first, heads, width):
    rows = query.shape[0]
    step = math.gcd(heads, 2 * LANES // math.gcd(width, LANES))
    start = first // step
    spec = pl.BlockSpec((rows, step * width), lambda i: (0, i + start))
    return pl.pallas_call(
        turn_in_kernel,
        grid=(heads // step,),
        in_specs=[spec] * 3,
        out_specs=pl.BlockSpec((step, 3, width, rows), lambda i: (i, 0, 0, 0)),
        out_shape=jax.ShapeDtypeStruct((heads, 3, width, rows), query.dtype),
        cost_estimate=pl.CostEstimate(
            flops=0, transcendentals=0, bytes_accessed=12 * heads * width * rows
        ),
        name="turn_in",
    )(query, key, value)


def turn_out_kernel(first, in_ref, *refs):
    out_ref, turned, sems = refs[-3:]
    heads, width, rows = in_ref.shape
    lots, _, span = turned.shape
    some = heads // lots
    copies = []
    for i in range(lots):
        turned[i] = in_ref[i * some : (i + 1) * some].reshape(span, rows).T
        columns = pl.ds(first * width + i * span, span)
        copies.append(pltpu.make_async_copy(turned.at[i], out_ref.at[:, columns], sems.at[i]))
        copies[-1].start()
    for copy in copies:
        copy.wait()


def turn_out(parts, first, so_far, heads_total):
    heads, width, rows = parts.shape
    lots = math.gcd(LOTS, heads * width // LANES)
    given = () if so_far is None else (so_far,)
    return pl.pallas_call(
        functools.partial(turn_out_kernel, first),
        in_specs=[pl.BlockSpec(memory_space=pltpu.VMEM)]
        + [pl.BlockSpec(memory_space=pl.ANY)] * len(given),
        out_specs=pl.BlockSpec(memory_space=pl.ANY),
        out_shape=jax.ShapeDtypeStruct((rows, heads_total * width), parts.dtype),
        input_output_aliases={1: 0} if given else {},
        scratch_shapes=[
            pltpu.VMEM((lots, rows, heads * width // lots), parts.dtype),
            pltpu.SemaphoreType.DMA((lots,)),
        ],
        cost_estimate=pl.CostEstimate(
            flops=0, transcendentals=0, bytes_accessed=4 * heads * width * rows
        ),
        name="turn_out",
    )(parts, *given)


def attend_kernel(sub, v_parts, parts_out, slope_ref, band_ref, given_ref, *refs):
    v_refs, out_refs, refs = refs[:v_parts], refs[v_parts : v_parts + parts_out], refs[v_parts + parts_out :]
    queries, keys, values, refs = refs[0], refs[1], refs[2], refs[3:]
    blocks, _, width, rows = given_ref.shape
    staged = refs if parts_out > 1 else ()
    qkv_ref = staged[0] if staged else given_ref
    out_ref = refs[-1] if parts_out > 1 else out_refs[0]
    seq, slot = lax.axis_index("seq"), lax.axis_index("head")
    slots = lax.axis_size("head")
    pad = LANES - width
    half = 2 * rows
    per = 2 * sub
    factor = LOG2E * width**-0.5
    slope = slope_ref[0]
    band = band_ref[0]

    row = lax.broadcasted_iota(jnp.int32, (pad, rows), 0)
    lane = lax.broadcasted_iota(jnp.int32, (pad, rows), 1)

    def fill(block, carry):
        at = pl.multiple_of(block * rows, rows)
        bias = (slope * width**0.5) * (at + lane).astype(jnp.float32)
        high = bias.astype(jnp.bfloat16).astype(jnp.float32)
        rest = bias - high
        middle = rest.astype(jnp.bfloat16).astype(jnp.float32)
        low = rest - middle
        part = jnp.where(
            (row == 0) | (row == 3), high, jnp.where((row == 1) | (row == 4), middle, low)
        )
        for_key = jnp.where(row < 3, part, jnp.where(row < 6, 1.0, 0.0)).astype(jnp.bfloat16)
        for_query = jnp.where(row < 3, 1.0, jnp.where(row < 6, -part, 0.0)).astype(jnp.bfloat16)
        keys[pl.ds(at, rows), :] = jnp.concatenate([qkv_ref[block, 1], for_key], axis=0).T
        queries[:width, pl.ds(at, rows)] = qkv_ref[block, 0]
        queries[width:, pl.ds(at, rows)] = for_query
        if not v_parts:
            values[:width, pl.ds(at, rows)] = qkv_ref[block, 2]
        values[width:, pl.ds(at, rows)] = jnp.ones((pad, rows), jnp.bfloat16)
        return carry

    if staged:
        lot = blocks // LOTS
        copies = []
        for i in range(LOTS):
            some = pl.ds(i * lot, lot)
            copies.append(
                pltpu.make_async_copy(given_ref.at[some], qkv_ref.at[some], staged[1].at[i])
            )
            copies[-1].start()
        for i in range(LOTS):
            copies[i].wait()
            lax.fori_loop(i * lot, (i + 1) * lot, fill, 0, unroll=4)
    else:
        lax.fori_loop(0, blocks, fill, 0, unroll=4)
    for flip, ref in enumerate(v_refs):
        for shift in range(slots):
            block = (seq ^ flip) * slots + (slot + slots - shift) % slots
            at = pl.multiple_of(block * rows, rows)
            values[:width, pl.ds(at, rows)] = ref[shift]

    def attend_tile(fast, index, carry):
        first = per * index

        def query_of(s):
            return queries[:, pl.ds(pl.multiple_of((first + 2 * s) * rows, half), half)]

        def scored(start, count, s, masked, query):
            score = jnp.dot(keys[pl.ds(start, count), :], query, preferred_element_type=jnp.float32)
            if not masked:
                return score
            key = lax.broadcasted_iota(jnp.int32, (count, half), 0)
            token = lax.broadcasted_iota(jnp.int32, (count, half), 1)
            if masked == "diagonal":
                live = token + (count - half) >= key
            else:
                ahead = (first + 2 * s) * rows - start
                live = (ahead // BLOCK + token // BLOCK) - key // BLOCK < band
            return jnp.where(live, score, DEAD)

        def weighed(start, count, weights):
            return jnp.dot(
                values[:, pl.ds(start, count)],
                weights.astype(jnp.bfloat16),
                preferred_element_type=jnp.float32,
            )

        def slow_step(start, count, s, masked, query, state):
            top, total = state
            score = scored(start, count, s, masked, query)
            new_top = jnp.maximum(top, jnp.max(score, axis=0, keepdims=True))
            weights = jnp.exp2(score * factor - new_top * factor)
            shrink = jnp.exp2((top - new_top) * factor)
            return new_top, total * shrink + weighed(start, count, weights)

        def fast_steps(start, counts, masked, query, states):
            pieces = [[] for _ in range(sub)]
            highs = [high for _, high in states]
            for at in range(0, max(counts), PIECE):
                for s in range(sub):
                    if at >= counts[s]:
                        continue
                    mask = masked
                    if masked == "diagonal" and at + PIECE < counts[s]:
                        mask = False
                    score = scored(start + at, PIECE, s, mask, query[s])
                    pieces[s].append(jnp.exp2(score * factor).astype(jnp.bfloat16))
                    top = jnp.max(score.reshape(PIECE // 8, 8, half), axis=0)
                    highs[s] = jnp.maximum(highs[s], top)
            weights = [jnp.concatenate(pieces[s], axis=0) for s in range(sub)]
            return [
                (states[s][0] + weighed(start, counts[s], weights[s]), highs[s])
                for s in range(sub)
            ]

        whole = jnp.minimum(first, band - per) // per
        needed = jnp.minimum(first, band - 1)
        rest = (needed - per * whole + per - 1) // per

        def sweep(steps, states):
            def body(masked):
                def some(j, states):
                    start = pl.multiple_of((first - per * (j + 1)) * rows, half)
                    return steps(start, [per * rows] * sub, masked, query, states)

                return some

            states = lax.fori_loop(0, whole, body(False), states)
            return lax.fori_loop(whole, whole + rest, body("band"), states)

        def finish(s, total):
            result = (total[:width] / total[width : width + 1]).astype(jnp.bfloat16)
            out_ref[first + 2 * s] = result[:, :rows]
            out_ref[first + 2 * s + 1] = result[:, rows:]

        def slow_steps(start, counts, masked, query, states):
            return [
                slow_step(start, counts[s], s, masked, query[s], states[s]) for s in range(sub)
            ]

        query = [query_of(s) for s in range(sub)]
        start = pl.multiple_of(first * rows, half)
        counts = [half * (s + 1) for s in range(sub)]
        nothing = jnp.zeros((LANES, half), jnp.float32)
        if fast:
            steps = fast_steps
            states = [(nothing, jnp.full((8, half), DEAD, jnp.float32))] * sub
        else:
            steps = slow_steps
            states = [(jnp.full((1, half), DEAD, jnp.float32), nothing)] * sub
        states = steps(start, counts, "diagonal", query, states)
        states = sweep(steps, states)
        for s in range(sub):
            finish(s, states[s][0 if fast else 1])
            if fast:
                high = jnp.max(states[s][1], axis=0, keepdims=True)
                carry = jnp.maximum(carry, jnp.abs(high))
        return carry

    worst = jnp.zeros((1, half), jnp.float32)
    worst = lax.fori_loop(0, blocks // per, functools.partial(attend_tile, True), worst)

    @pl.when(jnp.max(worst) * factor > SPAN)
    def _():
        lax.fori_loop(0, blocks // per, functools.partial(attend_tile, False), 0)

    if parts_out > 1:
        for flip, ref in enumerate(out_refs):
            ref[...] = out_ref[pl.ds((seq ^ flip) * slots, slots)]


def attend(given, slope, band, values=(), parts_out=1):
    blocks, _, width, rows = given.shape
    pairs = blocks * (blocks + 1) // 2
    sub = math.gcd(blocks, 8) // 2
    shape = (blocks // parts_out, width, rows)
    staged = [pltpu.VMEM(given.shape, given.dtype), pltpu.SemaphoreType.DMA((LOTS,))]
    results = pl.pallas_call(
        functools.partial(attend_kernel, sub, len(values), parts_out),
        in_specs=[
            pl.BlockSpec(memory_space=pltpu.SMEM),
            pl.BlockSpec(memory_space=pltpu.SMEM),
            pl.BlockSpec(memory_space=pltpu.VMEM if parts_out == 1 else pl.ANY),
        ]
        + [pl.BlockSpec(memory_space=pltpu.VMEM)] * len(values),
        out_specs=[pl.BlockSpec(memory_space=pltpu.VMEM)] * parts_out,
        out_shape=[jax.ShapeDtypeStruct(shape, given.dtype)] * parts_out,
        scratch_shapes=[
            pltpu.VMEM((LANES, blocks * rows), given.dtype),
            pltpu.VMEM((blocks * rows, LANES), given.dtype),
            pltpu.VMEM((LANES, blocks * rows), given.dtype),
        ]
        + (staged if parts_out > 1 else [])
        + ([pltpu.VMEM((blocks, width, rows), given.dtype)] if parts_out > 1 else []),
        compiler_params=pltpu.CompilerParams(vmem_limit_bytes=28 * 2**20),
        cost_estimate=pl.CostEstimate(
            flops=4 * pairs * rows * rows * LANES,
            transcendentals=pairs * rows * rows,
            bytes_accessed=8 * blocks * width * rows,
        ),
        name="attend",
    )(slope, band, given, *values)
    return results if parts_out > 1 else results[0]


def after(value, *others):
    return lax.optimization_barrier((value, *others))[0]


def moved(shapes, dtype, name, kernel, operands, scratch=(), where=None):
    specs = where or [pl.BlockSpec(memory_space=pltpu.VMEM)] * len(operands)
    size = 4 * sum(math.prod(shape) for shape in shapes)
    return pl.pallas_call(
        kernel,
        in_specs=specs,
        out_specs=[pl.BlockSpec(memory_space=pltpu.VMEM)] * len(shapes),
        out_shape=[jax.ShapeDtypeStruct(shape, dtype) for shape in shapes],
        scratch_shapes=list(scratch),
        cost_estimate=pl.CostEstimate(flops=0, transcendentals=0, bytes_accessed=size),
        name=name,
    )(*operands)


def cut_kernel(first, value_ref, *refs):
    outs, sems = refs[:-1], refs[-1]
    slot, slots = lax.axis_index("head"), lax.axis_size("head")
    span = outs[0].shape[1]
    copies = []
    for i, out in enumerate(outs):
        column = pl.multiple_of(first + ((slot + i + 1) % slots) * span, LANES)
        copies.append(pltpu.make_async_copy(value_ref.at[:, pl.ds(column, span)], out, sems.at[i]))
        copies[-1].start()
    for copy in copies:
        copy.wait()


def cut(value, first, span):
    slots = lax.axis_size("head")
    return moved(
        [(value.shape[0], span)] * (slots - 1),
        value.dtype,
        "cut",
        functools.partial(cut_kernel, first),
        [value],
        [pltpu.SemaphoreType.DMA((slots - 1,))],
        [pl.BlockSpec(memory_space=pl.ANY)],
    )


def turn_values_kernel(first, value_ref, *refs):
    slot, slots = lax.axis_index("head"), lax.axis_size("head")
    came, outs = refs[: slots - 1], refs[slots - 1 : -3]
    own, turned, sem = refs[-3:]
    span = own.shape[1]
    width = outs[0].shape[1]
    seq = lax.axis_index("seq")
    column = pl.multiple_of(first + slot * span, LANES)
    copy = pltpu.make_async_copy(value_ref.at[:, pl.ds(column, span)], own, sem)
    copy.start()
    for shift in [*range(1, slots), 0]:
        if shift == 0:
            copy.wait()
        turned[...] = (own if shift == 0 else came[shift - 1])[...].T
        for flip, out in enumerate(outs):
            at = pl.multiple_of((seq ^ flip) * width, 16)
            out[shift] = turned[pl.ds(at, width), :]


def turn_values(value, came, first, width):
    seqs, slots = lax.axis_size("seq"), lax.axis_size("head")
    rows, span = came[0].shape
    return moved(
        [(slots, width, rows)] * seqs,
        value.dtype,
        "turn_values",
        functools.partial(turn_values_kernel, first),
        [value, *came],
        [
            pltpu.VMEM((rows, span), value.dtype),
            pltpu.VMEM((span, rows), value.dtype),
            pltpu.SemaphoreType.DMA(()),
        ],
        [pl.BlockSpec(memory_space=pl.ANY)] + [pl.BlockSpec(memory_space=pltpu.VMEM)] * len(came),
    )


def regroup_kernel(*refs):
    seq, slot = lax.axis_index("seq"), lax.axis_index("head")
    seqs, slots = lax.axis_size("seq"), lax.axis_size("head")
    for flip in range(seqs):
        for shift in range(slots):
            refs[seqs + shift][seq ^ flip] = refs[flip][(slot + shift) % slots]


def regroup(came):
    seqs, slots = lax.axis_size("seq"), lax.axis_size("head")
    shape = (seqs, *came[0].shape[1:])
    return moved([shape] * slots, came[0].dtype, "regroup", regroup_kernel, came)


def turn_in_slots_kernel(arrays, *refs):
    out_ref = refs[-1]
    seqs, slots, _, width, rows = out_ref.shape
    for which in range(arrays):
        turned = refs[which][...].T
        for slot in range(slots):
            for seq in range(seqs):
                at = (slot * seqs + seq) * width
                out_ref[seq, slot, which] = turned[at : at + width]


def turn_in_slots(arrays, first, width):
    seqs, slots = lax.axis_size("seq"), lax.axis_size("head")
    rows = arrays[0].shape[0]
    step = math.gcd(slots, 2)
    start = first // (step * seqs)
    spec = pl.BlockSpec((rows, step * seqs * width), lambda i: (0, i + start))
    count = len(arrays)
    out = pl.pallas_call(
        functools.partial(turn_in_slots_kernel, count),
        grid=(slots // step,),
        in_specs=[spec] * count,
        out_specs=pl.BlockSpec((seqs, step, count, width, rows), lambda i: (0, i, 0, 0, 0)),
        out_shape=jax.ShapeDtypeStruct((seqs, slots, count, width, rows), arrays[0].dtype),
        cost_estimate=pl.CostEstimate(
            flops=0,
            transcendentals=0,
            bytes_accessed=4 * count * seqs * slots * width * rows,
        ),
        compiler_params=pltpu.CompilerParams(vmem_limit_bytes=WHOLE_VMEM),
        name="turn_in_slots",
    )(*arrays)
    return out.reshape(seqs * slots, count, width, rows)


def turn_out_slots_kernel(first, parts, *refs):
    out_ref, turned, sems = refs[-3:]
    slots, rows, span = turned.shape
    slot = lax.axis_index("head")
    copies = []
    for i in range(slots):
        if parts == 1:
            _, width, _ = refs[0].shape
            heads = [refs[0][seq * slots + i] for seq in range(span // width)]
            some, owner = jnp.concatenate(heads, axis=0), i
        else:
            some, owner = refs[i][...].reshape(span, rows), (slot + slots - i) % slots
        turned[i] = some.T
        columns = pl.ds(pl.multiple_of(first + owner * span, LANES), span)
        copies.append(pltpu.make_async_copy(turned.at[i], out_ref.at[:, columns], sems.at[i]))
        copies[-1].start()
    for copy in copies:
        copy.wait()


def turn_out_slots(parts, first, so_far, width_total):
    slots = lax.axis_size("head")
    rows = parts[0].shape[-1]
    span = sum(math.prod(part.shape[:-1]) for part in parts) // slots
    given = () if so_far is None else (so_far,)
    return pl.pallas_call(
        functools.partial(turn_out_slots_kernel, first, len(parts)),
        in_specs=[pl.BlockSpec(memory_space=pltpu.VMEM)] * len(parts)
        + [pl.BlockSpec(memory_space=pl.ANY)] * len(given),
        out_specs=pl.BlockSpec(memory_space=pl.ANY),
        out_shape=jax.ShapeDtypeStruct((rows, width_total), parts[0].dtype),
        input_output_aliases={len(parts): 0} if given else {},
        scratch_shapes=[
            pltpu.VMEM((slots, rows, span), parts[0].dtype),
            pltpu.SemaphoreType.DMA((slots,)),
        ],
        cost_estimate=pl.CostEstimate(
            flops=0 if so_far is not None else BESIDE * 10**9,
            transcendentals=0,
            bytes_accessed=4 * slots * span * rows,
        ),
        name="turn_out_slots",
    )(*parts, *given)


def in_two_sets(query, key, value, slope, band, width):
    seqs, slots = lax.axis_size("seq"), lax.axis_size("head")
    seq, slot = lax.axis_index("seq"), lax.axis_index("head")
    half = seqs * slots
    span = seqs * width

    def send(x, flip, shift):
        to = [
            (s * slots + z, (s ^ flip) * slots + (z + shift) % slots)
            for s in range(seqs)
            for z in range(slots)
        ]
        return x if flip == shift == 0 else lax.ppermute(x, AXES, to)

    def mine(first):
        head = first + slot * seqs + seq
        return [lax.dynamic_slice_in_dim(x, head, 1) for x in (slope, band)]

    raw = (query, key, value)
    given_a = lax.all_to_all(turn_in_slots(raw, 0, width), AXES, 0, 0, tiled=True)
    given_b = lax.all_to_all(turn_in_slots(raw, half, width), AXES, 0, 0, tiled=True)

    result_a = attend(given_a, *mine(0), parts_out=seqs)
    groups = regroup([send(x, flip, 0) for flip, x in enumerate(result_a)])
    *groups, given_b = lax.optimization_barrier((*groups, given_b))
    back_a = [send(x, 0, shift) for shift, x in enumerate(groups)]

    result_b = attend(given_b, *mine(half))
    back_b = lax.all_to_all(result_b, AXES, 0, 0, tiled=True)
    out = turn_out_slots(back_a, 0, None, 2 * half * width)
    return turn_out_slots([back_b], half * width, out, 2 * half * width)


def on_device(query, key, value, exponent):
    rows, width_total = query.shape
    heads = exponent.shape[0]
    width = width_total // heads
    seqs, slots = lax.axis_size("seq"), lax.axis_size("head")
    devices = seqs * slots

    band = MIN_BAND + (exponent - 1) * (MAX_BAND - MIN_BAND) // (heads - 1)
    slope = jnp.exp2(-12.0 * exponent.astype(jnp.float32) / heads)

    two_each = heads == 2 * devices and seqs & (seqs - 1) == 0 and slots % 2 == 0
    if two_each and seqs * width % LANES == 0:
        return in_two_sets(query, key, value, slope, band, width)

    me = lax.axis_index("seq") * slots + lax.axis_index("head")
    share = max(1, devices // heads)
    owners = devices // share
    out = None
    for part in range(heads // owners):
        sent = turn_in(query, key, value, part * owners, owners, width)
        if share > 1:
            sent = jnp.repeat(sent, share, axis=0)
        given = lax.all_to_all(sent, AXES, 0, 0, tiled=True)
        head = part * owners + me // share
        mine = [lax.dynamic_slice_in_dim(x, head, 1) for x in (slope, band)]
        result = attend(given, *mine)
        back = lax.all_to_all(result, AXES, 0, 0, tiled=True)
        if share > 1:
            back = back.reshape(owners, share, width, rows)[:, 0]
        out = turn_out(back, part * owners, out, heads)
    return out


def solution(mesh):
    spec = P(AXES, None)
    return jax.shard_map(
        on_device,
        mesh=mesh,
        in_specs=(spec, spec, spec, P()),
        out_specs=spec,
        check_vma=False,
    )
```

```python
import functools
import math

import jax
import jax.numpy as jnp
from jax import lax
from jax.experimental import pallas as pl
from jax.experimental.pallas import tpu as pltpu
from jax.sharding import PartitionSpec as P

BLOCK = 128
MIN_BAND = 16
MAX_BAND = 40
AXES = ("seq", "head")
LANES = 128
DEAD = -1e30
LOG2E = 1.4426950408889634
PIECE = 256
SPAN = 90.0
BESIDE = 400
WHOLE_VMEM = 62 * 2**20
LOTS = 4


def turn_in_kernel(q_ref, k_ref, v_ref, out_ref):
    heads, _, width, rows = out_ref.shape
    for which, ref in enumerate((q_ref, k_ref, v_ref)):
        turned = ref[...].T
        for head in range(heads):
            out_ref[head, which] = turned[head * width : (head + 1) * width]


def turn_in(query, key, value, first, heads, width):
    rows = query.shape[0]
    step = math.gcd(heads, 2 * LANES // math.gcd(width, LANES))
    start = first // step
    spec = pl.BlockSpec((rows, step * width), lambda i: (0, i + start))
    return pl.pallas_call(
        turn_in_kernel,
        grid=(heads // step,),
        in_specs=[spec] * 3,
        out_specs=pl.BlockSpec((step, 3, width, rows), lambda i: (i, 0, 0, 0)),
        out_shape=jax.ShapeDtypeStruct((heads, 3, width, rows), query.dtype),
        cost_estimate=pl.CostEstimate(
            flops=0, transcendentals=0, bytes_accessed=12 * heads * width * rows
        ),
        name="turn_in",
    )(query, key, value)


def turn_out_kernel(first, in_ref, *refs):
    out_ref, turned, sems = refs[-3:]
    heads, width, rows = in_ref.shape
    lots, _, span = turned.shape
    some = heads // lots
    copies = []
    for i in range(lots):
        turned[i] = in_ref[i * some : (i + 1) * some].reshape(span, rows).T
        columns = pl.ds(first * width + i * span, span)
        copies.append(pltpu.make_async_copy(turned.at[i], out_ref.at[:, columns], sems.at[i]))
        copies[-1].start()
    for copy in copies:
        copy.wait()


def turn_out(parts, first, so_far, heads_total):
    heads, width, rows = parts.shape
    lots = math.gcd(LOTS, heads * width // LANES)
    given = () if so_far is None else (so_far,)
    return pl.pallas_call(
        functools.partial(turn_out_kernel, first),
        in_specs=[pl.BlockSpec(memory_space=pltpu.VMEM)]
        + [pl.BlockSpec(memory_space=pl.ANY)] * len(given),
        out_specs=pl.BlockSpec(memory_space=pl.ANY),
        out_shape=jax.ShapeDtypeStruct((rows, heads_total * width), parts.dtype),
        input_output_aliases={1: 0} if given else {},
        scratch_shapes=[
            pltpu.VMEM((lots, rows, heads * width // lots), parts.dtype),
            pltpu.SemaphoreType.DMA((lots,)),
        ],
        cost_estimate=pl.CostEstimate(
            flops=0, transcendentals=0, bytes_accessed=4 * heads * width * rows
        ),
        name="turn_out",
    )(parts, *given)


def attend_kernel(sub, v_parts, parts_out, slope_ref, band_ref, given_ref, *refs):
    v_refs, out_refs, refs = refs[:v_parts], refs[v_parts : v_parts + parts_out], refs[v_parts + parts_out :]
    queries, keys, values, refs = refs[0], refs[1], refs[2], refs[3:]
    blocks, _, width, rows = given_ref.shape
    staged = refs if parts_out > 1 else ()
    qkv_ref = staged[0] if staged else given_ref
    out_ref = refs[-1] if parts_out > 1 else out_refs[0]
    seq, slot = lax.axis_index("seq"), lax.axis_index("head")
    slots = lax.axis_size("head")
    pad = LANES - width
    half = 2 * rows
    per = 2 * sub
    factor = LOG2E * width**-0.5
    slope = slope_ref[0]
    band = band_ref[0]

    row = lax.broadcasted_iota(jnp.int32, (pad, rows), 0)
    lane = lax.broadcasted_iota(jnp.int32, (pad, rows), 1)

    def fill(block, carry):
        at = pl.multiple_of(block * rows, rows)
        bias = (slope * width**0.5) * (at + lane).astype(jnp.float32)
        high = bias.astype(jnp.bfloat16).astype(jnp.float32)
        rest = bias - high
        middle = rest.astype(jnp.bfloat16).astype(jnp.float32)
        low = rest - middle
        part = jnp.where(
            (row == 0) | (row == 3), high, jnp.where((row == 1) | (row == 4), middle, low)
        )
        for_key = jnp.where(row < 3, part, jnp.where(row < 6, 1.0, 0.0)).astype(jnp.bfloat16)
        for_query = jnp.where(row < 3, 1.0, jnp.where(row < 6, -part, 0.0)).astype(jnp.bfloat16)
        keys[pl.ds(at, rows), :] = jnp.concatenate([qkv_ref[block, 1], for_key], axis=0).T
        queries[:width, pl.ds(at, rows)] = qkv_ref[block, 0]
        queries[width:, pl.ds(at, rows)] = for_query
        if not v_parts:
            values[:width, pl.ds(at, rows)] = qkv_ref[block, 2]
        values[width:, pl.ds(at, rows)] = jnp.ones((pad, rows), jnp.bfloat16)
        return carry

    if staged:
        lot = blocks // LOTS
        copies = []
        for i in range(LOTS):
            some = pl.ds(i * lot, lot)
            copies.append(
                pltpu.make_async_copy(given_ref.at[some], qkv_ref.at[some], staged[1].at[i])
            )
            copies[-1].start()
        for i in range(LOTS):
            copies[i].wait()
            lax.fori_loop(i * lot, (i + 1) * lot, fill, 0, unroll=4)
    else:
        lax.fori_loop(0, blocks, fill, 0, unroll=4)
    for flip, ref in enumerate(v_refs):
        for shift in range(slots):
            block = (seq ^ flip) * slots + (slot + slots - shift) % slots
            at = pl.multiple_of(block * rows, rows)
            values[:width, pl.ds(at, rows)] = ref[shift]

    def attend_tile(fast, index, carry):
        first = per * index

        def query_of(s):
            return queries[:, pl.ds(pl.multiple_of((first + 2 * s) * rows, half), half)]

        def scored(start, count, s, masked, query):
            score = jnp.dot(keys[pl.ds(start, count), :], query, preferred_element_type=jnp.float32)
            if not masked:
                return score
            key = lax.broadcasted_iota(jnp.int32, (count, half), 0)
            token = lax.broadcasted_iota(jnp.int32, (count, half), 1)
            if masked == "diagonal":
                live = token + (count - half) >= key
            else:
                ahead = (first + 2 * s) * rows - start
                live = (ahead // BLOCK + token // BLOCK) - key // BLOCK < band
            return jnp.where(live, score, DEAD)

        def weighed(start, count, weights):
            return jnp.dot(
                values[:, pl.ds(start, count)],
                weights.astype(jnp.bfloat16),
                preferred_element_type=jnp.float32,
            )

        def slow_step(start, count, s, masked, query, state):
            top, total = state
            score = scored(start, count, s, masked, query)
            new_top = jnp.maximum(top, jnp.max(score, axis=0, keepdims=True))
            weights = jnp.exp2(score * factor - new_top * factor)
            shrink = jnp.exp2((top - new_top) * factor)
            return new_top, total * shrink + weighed(start, count, weights)

        def fast_steps(start, counts, masked, query, states):
            pieces = [[] for _ in range(sub)]
            highs = [high for _, high in states]
            for at in range(0, max(counts), PIECE):
                for s in range(sub):
                    if at >= counts[s]:
                        continue
                    mask = masked
                    if masked == "diagonal" and at + PIECE < counts[s]:
                        mask = False
                    score = scored(start + at, PIECE, s, mask, query[s])
                    pieces[s].append(jnp.exp2(score * factor).astype(jnp.bfloat16))
                    top = jnp.max(score.reshape(PIECE // 8, 8, half), axis=0)
                    highs[s] = jnp.maximum(highs[s], top)
            weights = [jnp.concatenate(pieces[s], axis=0) for s in range(sub)]
            return [
                (states[s][0] + weighed(start, counts[s], weights[s]), highs[s])
                for s in range(sub)
            ]

        whole = jnp.minimum(first, band - per) // per
        needed = jnp.minimum(first, band - 1)
        rest = (needed - per * whole + per - 1) // per

        def sweep(steps, states):
            def body(masked):
                def some(j, states):
                    start = pl.multiple_of((first - per * (j + 1)) * rows, half)
                    return steps(start, [per * rows] * sub, masked, query, states)

                return some

            states = lax.fori_loop(0, whole, body(False), states)
            return lax.fori_loop(whole, whole + rest, body("band"), states)

        def finish(s, total):
            result = (total[:width] * (1.0 / total[width : width + 1])).astype(jnp.bfloat16)
            out_ref[first + 2 * s] = result[:, :rows]
            out_ref[first + 2 * s + 1] = result[:, rows:]

        def slow_steps(start, counts, masked, query, states):
            return [
                slow_step(start, counts[s], s, masked, query[s], states[s]) for s in range(sub)
            ]

        query = [query_of(s) for s in range(sub)]
        start = pl.multiple_of(first * rows, half)
        counts = [half * (s + 1) for s in range(sub)]
        nothing = jnp.zeros((LANES, half), jnp.float32)
        if fast:
            steps = fast_steps
            states = [(nothing, jnp.full((8, half), DEAD, jnp.float32))] * sub
        else:
            steps = slow_steps
            states = [(jnp.full((1, half), DEAD, jnp.float32), nothing)] * sub
        states = steps(start, counts, "diagonal", query, states)
        states = sweep(steps, states)
        for s in range(sub):
            finish(s, states[s][0 if fast else 1])
            if fast:
                high = jnp.max(states[s][1], axis=0, keepdims=True)
                carry = jnp.maximum(carry, jnp.abs(high))
        return carry

    worst = jnp.zeros((1, half), jnp.float32)
    worst = lax.fori_loop(0, blocks // per, functools.partial(attend_tile, True), worst)

    @pl.when(jnp.max(worst) * factor > SPAN)
    def _():
        lax.fori_loop(0, blocks // per, functools.partial(attend_tile, False), 0)

    if parts_out > 1:
        for flip, ref in enumerate(out_refs):
            ref[...] = out_ref[pl.ds((seq ^ flip) * slots, slots)]


def attend(given, slope, band, values=(), parts_out=1):
    blocks, _, width, rows = given.shape
    pairs = blocks * (blocks + 1) // 2
    sub = math.gcd(blocks, 8) // 2
    shape = (blocks // parts_out, width, rows)
    staged = [pltpu.VMEM(given.shape, given.dtype), pltpu.SemaphoreType.DMA((LOTS,))]
    results = pl.pallas_call(
        functools.partial(attend_kernel, sub, len(values), parts_out),
        in_specs=[
            pl.BlockSpec(memory_space=pltpu.SMEM),
            pl.BlockSpec(memory_space=pltpu.SMEM),
            pl.BlockSpec(memory_space=pltpu.VMEM if parts_out == 1 else pl.ANY),
        ]
        + [pl.BlockSpec(memory_space=pltpu.VMEM)] * len(values),
        out_specs=[pl.BlockSpec(memory_space=pltpu.VMEM)] * parts_out,
        out_shape=[jax.ShapeDtypeStruct(shape, given.dtype)] * parts_out,
        scratch_shapes=[
            pltpu.VMEM((LANES, blocks * rows), given.dtype),
            pltpu.VMEM((blocks * rows, LANES), given.dtype),
            pltpu.VMEM((LANES, blocks * rows), given.dtype),
        ]
        + (staged if parts_out > 1 else [])
        + ([pltpu.VMEM((blocks, width, rows), given.dtype)] if parts_out > 1 else []),
        compiler_params=pltpu.CompilerParams(vmem_limit_bytes=28 * 2**20),
        cost_estimate=pl.CostEstimate(
            flops=4 * pairs * rows * rows * LANES,
            transcendentals=pairs * rows * rows,
            bytes_accessed=8 * blocks * width * rows,
        ),
        name="attend",
    )(slope, band, given, *values)
    return results if parts_out > 1 else results[0]


def after(value, *others):
    return lax.optimization_barrier((value, *others))[0]


def moved(shapes, dtype, name, kernel, operands, scratch=(), where=None):
    specs = where or [pl.BlockSpec(memory_space=pltpu.VMEM)] * len(operands)
    size = 4 * sum(math.prod(shape) for shape in shapes)
    return pl.pallas_call(
        kernel,
        in_specs=specs,
        out_specs=[pl.BlockSpec(memory_space=pltpu.VMEM)] * len(shapes),
        out_shape=[jax.ShapeDtypeStruct(shape, dtype) for shape in shapes],
        scratch_shapes=list(scratch),
        cost_estimate=pl.CostEstimate(flops=0, transcendentals=0, bytes_accessed=size),
        name=name,
    )(*operands)


def cut_kernel(first, value_ref, *refs):
    outs, sems = refs[:-1], refs[-1]
    slot, slots = lax.axis_index("head"), lax.axis_size("head")
    span = outs[0].shape[1]
    copies = []
    for i, out in enumerate(outs):
        column = pl.multiple_of(first + ((slot + i + 1) % slots) * span, LANES)
        copies.append(pltpu.make_async_copy(value_ref.at[:, pl.ds(column, span)], out, sems.at[i]))
        copies[-1].start()
    for copy in copies:
        copy.wait()


def cut(value, first, span):
    slots = lax.axis_size("head")
    return moved(
        [(value.shape[0], span)] * (slots - 1),
        value.dtype,
        "cut",
        functools.partial(cut_kernel, first),
        [value],
        [pltpu.SemaphoreType.DMA((slots - 1,))],
        [pl.BlockSpec(memory_space=pl.ANY)],
    )


def turn_values_kernel(first, value_ref, *refs):
    slot, slots = lax.axis_index("head"), lax.axis_size("head")
    came, outs = refs[: slots - 1], refs[slots - 1 : -3]
    own, turned, sem = refs[-3:]
    span = own.shape[1]
    width = outs[0].shape[1]
    seq = lax.axis_index("seq")
    column = pl.multiple_of(first + slot * span, LANES)
    copy = pltpu.make_async_copy(value_ref.at[:, pl.ds(column, span)], own, sem)
    copy.start()
    for shift in [*range(1, slots), 0]:
        if shift == 0:
            copy.wait()
        turned[...] = (own if shift == 0 else came[shift - 1])[...].T
        for flip, out in enumerate(outs):
            at = pl.multiple_of((seq ^ flip) * width, 16)
            out[shift] = turned[pl.ds(at, width), :]


def turn_values(value, came, first, width):
    seqs, slots = lax.axis_size("seq"), lax.axis_size("head")
    rows, span = came[0].shape
    return moved(
        [(slots, width, rows)] * seqs,
        value.dtype,
        "turn_values",
        functools.partial(turn_values_kernel, first),
        [value, *came],
        [
            pltpu.VMEM((rows, span), value.dtype),
            pltpu.VMEM((span, rows), value.dtype),
            pltpu.SemaphoreType.DMA(()),
        ],
        [pl.BlockSpec(memory_space=pl.ANY)] + [pl.BlockSpec(memory_space=pltpu.VMEM)] * len(came),
    )


def regroup_kernel(*refs):
    seq, slot = lax.axis_index("seq"), lax.axis_index("head")
    seqs, slots = lax.axis_size("seq"), lax.axis_size("head")
    for flip in range(seqs):
        for shift in range(slots):
            refs[seqs + shift][seq ^ flip] = refs[flip][(slot + shift) % slots]


def regroup(came):
    seqs, slots = lax.axis_size("seq"), lax.axis_size("head")
    shape = (seqs, *came[0].shape[1:])
    return moved([shape] * slots, came[0].dtype, "regroup", regroup_kernel, came)


def turn_in_slots_kernel(arrays, *refs):
    out_ref = refs[-1]
    seqs, slots, _, width, rows = out_ref.shape
    for which in range(arrays):
        turned = refs[which][...].T
        for slot in range(slots):
            for seq in range(seqs):
                at = (slot * seqs + seq) * width
                out_ref[seq, slot, which] = turned[at : at + width]


def turn_in_slots(arrays, first, width):
    seqs, slots = lax.axis_size("seq"), lax.axis_size("head")
    rows = arrays[0].shape[0]
    step = math.gcd(slots, 2)
    start = first // (step * seqs)
    spec = pl.BlockSpec((rows, step * seqs * width), lambda i: (0, i + start))
    count = len(arrays)
    out = pl.pallas_call(
        functools.partial(turn_in_slots_kernel, count),
        grid=(slots // step,),
        in_specs=[spec] * count,
        out_specs=pl.BlockSpec((seqs, step, count, width, rows), lambda i: (0, i, 0, 0, 0)),
        out_shape=jax.ShapeDtypeStruct((seqs, slots, count, width, rows), arrays[0].dtype),
        cost_estimate=pl.CostEstimate(
            flops=0,
            transcendentals=0,
            bytes_accessed=4 * count * seqs * slots * width * rows,
        ),
        compiler_params=pltpu.CompilerParams(vmem_limit_bytes=WHOLE_VMEM),
        name="turn_in_slots",
    )(*arrays)
    return out.reshape(seqs * slots, count, width, rows)


def turn_out_slots_kernel(first, parts, *refs):
    out_ref, turned, sems = refs[-3:]
    slots, rows, span = turned.shape
    slot = lax.axis_index("head")
    copies = []
    for i in range(slots):
        if parts == 1:
            _, width, _ = refs[0].shape
            heads = [refs[0][seq * slots + i] for seq in range(span // width)]
            some, owner = jnp.concatenate(heads, axis=0), i
        else:
            some, owner = refs[i][...].reshape(span, rows), (slot + slots - i) % slots
        turned[i] = some.T
        columns = pl.ds(pl.multiple_of(first + owner * span, LANES), span)
        copies.append(pltpu.make_async_copy(turned.at[i], out_ref.at[:, columns], sems.at[i]))
        copies[-1].start()
    for copy in copies:
        copy.wait()


def turn_out_slots(parts, first, so_far, width_total):
    slots = lax.axis_size("head")
    rows = parts[0].shape[-1]
    span = sum(math.prod(part.shape[:-1]) for part in parts) // slots
    given = () if so_far is None else (so_far,)
    return pl.pallas_call(
        functools.partial(turn_out_slots_kernel, first, len(parts)),
        in_specs=[pl.BlockSpec(memory_space=pltpu.VMEM)] * len(parts)
        + [pl.BlockSpec(memory_space=pl.ANY)] * len(given),
        out_specs=pl.BlockSpec(memory_space=pl.ANY),
        out_shape=jax.ShapeDtypeStruct((rows, width_total), parts[0].dtype),
        input_output_aliases={len(parts): 0} if given else {},
        scratch_shapes=[
            pltpu.VMEM((slots, rows, span), parts[0].dtype),
            pltpu.SemaphoreType.DMA((slots,)),
        ],
        cost_estimate=pl.CostEstimate(
            flops=0 if so_far is not None else BESIDE * 10**9,
            transcendentals=0,
            bytes_accessed=4 * slots * span * rows,
        ),
        name="turn_out_slots",
    )(*parts, *given)


def in_two_sets(query, key, value, slope, band, width):
    seqs, slots = lax.axis_size("seq"), lax.axis_size("head")
    seq, slot = lax.axis_index("seq"), lax.axis_index("head")
    half = seqs * slots
    span = seqs * width

    def send(x, flip, shift):
        to = [
            (s * slots + z, (s ^ flip) * slots + (z + shift) % slots)
            for s in range(seqs)
            for z in range(slots)
        ]
        return x if flip == shift == 0 else lax.ppermute(x, AXES, to)

    def mine(first):
        head = first + slot * seqs + seq
        return [lax.dynamic_slice_in_dim(x, head, 1) for x in (slope, band)]

    raw = (query, key, value)
    given_a = lax.all_to_all(turn_in_slots(raw, 0, width), AXES, 0, 0, tiled=True)
    given_b = lax.all_to_all(turn_in_slots(raw, half, width), AXES, 0, 0, tiled=True)

    result_a = attend(given_a, *mine(0), parts_out=seqs)
    groups = regroup([send(x, flip, 0) for flip, x in enumerate(result_a)])
    held, given_b = lax.optimization_barrier((groups[2], given_b))
    groups = [*groups[:2], held, *groups[3:]]
    back_a = [send(x, 0, shift) for shift, x in enumerate(groups)]

    result_b = attend(given_b, *mine(half))
    back_b = lax.all_to_all(result_b, AXES, 0, 0, tiled=True)
    out = turn_out_slots(back_a, 0, None, 2 * half * width)
    return turn_out_slots([back_b], half * width, out, 2 * half * width)


def on_device(query, key, value, exponent):
    rows, width_total = query.shape
    heads = exponent.shape[0]
    width = width_total // heads
    seqs, slots = lax.axis_size("seq"), lax.axis_size("head")
    devices = seqs * slots

    band = MIN_BAND + (exponent - 1) * (MAX_BAND - MIN_BAND) // (heads - 1)
    slope = jnp.exp2(-12.0 * exponent.astype(jnp.float32) / heads)

    two_each = heads == 2 * devices and seqs & (seqs - 1) == 0 and slots % 2 == 0
    if two_each and seqs * width % LANES == 0:
        return in_two_sets(query, key, value, slope, band, width)

    me = lax.axis_index("seq") * slots + lax.axis_index("head")
    share = max(1, devices // heads)
    owners = devices // share
    out = None
    for part in range(heads // owners):
        sent = turn_in(query, key, value, part * owners, owners, width)
        if share > 1:
            sent = jnp.repeat(sent, share, axis=0)
        given = lax.all_to_all(sent, AXES, 0, 0, tiled=True)
        head = part * owners + me // share
        mine = [lax.dynamic_slice_in_dim(x, head, 1) for x in (slope, band)]
        result = attend(given, *mine)
        back = lax.all_to_all(result, AXES, 0, 0, tiled=True)
        if share > 1:
            back = back.reshape(owners, share, width, rows)[:, 0]
        out = turn_out(back, part * owners, out, heads)
    return out


def solution(mesh):
    spec = P(AXES, None)
    return jax.shard_map(
        on_device,
        mesh=mesh,
        in_specs=(spec, spec, spec, P()),
        out_specs=spec,
        check_vma=False,
    )
```
